512 devices in a mesh: dp: 512 (over x, z, y, core).
Axes of the slice: x: 4, y: 4, z: 16, core: 2. Of those that a mesh axis runs over, the one named last changes fastest.
Arguments:
- image: bfloat16 [196608, 1152], P('dp'), may hold values from -2 to 2
- text: bfloat16 [196608, 1152], P('dp'), may hold values from -2 to 2
- text_in: bfloat16 [196608, 576], P('dp'), may hold values from -0.015625 to 0.015625
- log_scale: float32 [1], replicated, may hold values from 1.5 to 2.5
- bias: float32 [1], replicated, may hold values from -4 to -1
Outputs:
- image_grad: bfloat16 [196608, 1152], P('dp')
- text_grad: bfloat16 [196608, 1152], P('dp')
- head_grad: bfloat16 [576, 576], replicated
The draws below stay inside these ranges and needn't reach their ends.
All inputs are finite; a program needn't handle non-finite values.
Results may differ from the reference program's by a relative error of at most 0.0065.
Values may be sent and summed in bfloat16 or wider, within the bound.
A program may use at most 64 MiB of HBM per device.

```python
import jax
import jax.numpy as jnp
from jax import lax

D = 1152
HIN = 576
HOUT = 576
ROWS = 384
REACH = 2
TOKENS = 196608


def shared_rows(key):
    return jax.random.normal(key, (TOKENS, D), jnp.float32)


def finish_rows(key, mixed):
    return jnp.clip(0.02 * mixed, -2.0, 2.0).astype(jnp.bfloat16)


def draw_image(key, part):
    base = shared_rows(key)
    key = jax.random.fold_in(key, 11)
    mixed = base + 0.8 * jax.random.normal(key, (TOKENS, D), jnp.float32)
    return finish_rows(key, mixed)


def draw_text(key, part):
    base = shared_rows(key)
    key = jax.random.fold_in(key, 13)
    mixed = base + 0.8 * jax.random.normal(key, (TOKENS, D), jnp.float32)
    return finish_rows(key, mixed)


def shard_levels(rng, dims, shards, smallest, top_value):
    def one(dim, parts):
        heights = jax.random.uniform(jax.random.fold_in(jax.random.fold_in(rng, 6), dim), (parts,), jnp.float32, smallest / len(shards), top_value / len(shards))
        return jnp.repeat(jnp.exp(heights), dims[dim] // parts).reshape((-1,) + (1,) * (len(dims) - dim - 1))

    loudness = one(*shards[0])
    for cut in shards[1:]:
        loudness = loudness * one(*cut)
    return loudness


def gaussian(stream_key, dims, deviation, most, pieces=(), held_as=jnp.bfloat16):
    level = shard_levels(stream_key, dims, pieces, -0.22, 0.18) if pieces else 1.0
    values = jax.random.normal(stream_key, dims, jnp.float32) * deviation * level
    return jnp.minimum(jnp.maximum(values, -most), most).astype(held_as)


def setup_inputs(seed: int = 0) -> dict:
    splits = jax.random.split(jax.random.key(seed), 6)
    image = draw_image(jax.random.fold_in(splits[5], 71), 0)
    text = draw_text(jax.random.fold_in(splits[5], 71), 0)
    text_in = gaussian(splits[2], (TOKENS, HIN), 0.003, 0.015625, ((0, 512),))
    log_scale = jnp.clip(jax.random.uniform(splits[3], (1,), jnp.float32, 1.5, 2.5), 1.5, 2.5)
    bias = jnp.clip(jax.random.uniform(splits[4], (1,), jnp.float32, -4.0, -1.0), -4.0, -1.0)
    return {"image": image, "text": text, "text_in": text_in, "log_scale": log_scale, "bias": bias}


EPS = 1e-06

def unit_rows(values):
    wide = values.astype(jnp.float32)
    inverse = lax.rsqrt(lax.optimization_barrier(jnp.sum(wide * wide, axis=-1, keepdims=True)) + EPS)
    return (wide * inverse, inverse)

def reference(image, text, text_in, log_scale, bias):
    logit_scale = jnp.exp(log_scale[0])
    logit_bias = bias[0]
    unit_img, inv_img = unit_rows(image)
    unit_txt, inv_txt = unit_rows(text)
    blocks = image.shape[0] // ROWS
    img_low = lax.optimization_barrier(unit_img.astype(jnp.bfloat16))
    txt_low = lax.optimization_barrier(unit_txt.astype(jnp.bfloat16))
    img_blocks = img_low.astype(jnp.float32).reshape(blocks, ROWS, -1)
    txt_blocks = txt_low.astype(jnp.float32).reshape(blocks, ROWS, -1)
    identity = jnp.eye(ROWS, dtype=jnp.float32)
    grad_img = jnp.zeros_like(img_blocks)
    grad_txt = jnp.zeros_like(txt_blocks)
    for offset in range(-REACH, REACH + 1):
        partner = jnp.roll(txt_blocks, -offset, axis=0)
        logits = logit_scale * jnp.einsum('bid,bjd->bij', img_blocks, partner) + logit_bias
        tile_grad = jax.nn.sigmoid(logits)
        if offset == 0:
            tile_grad = tile_grad - identity
        tile_low = lax.optimization_barrier(tile_grad.astype(jnp.bfloat16))
        tile_grad = tile_low.astype(jnp.float32)
        grad_img = grad_img + jnp.einsum('bij,bjd->bid', tile_grad, partner)
        grad_txt = grad_txt + jnp.roll(jnp.einsum('bij,bid->bjd', tile_grad, img_blocks), offset, axis=0)
    grad_img = logit_scale * grad_img.reshape(image.shape)
    grad_txt = logit_scale * grad_txt.reshape(text.shape)
    image_grad = ((grad_img - unit_img * lax.optimization_barrier(jnp.sum(unit_img * grad_img, axis=-1, keepdims=True))) * inv_img).astype(jnp.bfloat16)
    text_grad = ((grad_txt - unit_txt * lax.optimization_barrier(jnp.sum(unit_txt * grad_txt, axis=-1, keepdims=True))) * inv_txt).astype(jnp.bfloat16)
    head_grad = jnp.dot(text_in.T, text_grad[:, :HOUT], preferred_element_type=jnp.float32).astype(jnp.bfloat16)
    return (image_grad, text_grad, head_grad)
```

```python
import functools

import jax
import jax.numpy as jnp
from jax import lax
from jax.experimental import pallas as pl
from jax.experimental.pallas import tpu as pltpu
from jax.sharding import PartitionSpec as P

D = 1152
HIN = 576
HOUT = 576
ROWS = 384
EPS = 1e-06

NX, NZ, NY = 4, 16, 4
CHIPS = NX * NZ * NY
NCH = 4
CH = ROWS // NCH
HALF = HIN // 2
WIDE = 640
PIECE = 336
OWNERS = 11
ZROWS = 32
PADDED = OWNERS * ZROWS

MESH = pl.DeviceIdType.MESH
BF16 = jnp.bfloat16
F32 = jnp.float32


def remote(src, dst, send, recv, device):
    return pltpu.make_async_remote_copy(
        src_ref=src, dst_ref=dst, send_sem=send, recv_sem=recv,
        device_id=(device,), device_id_type=MESH,
    )


def at(x, z, y, core):
    return ((x * NZ + z) * NY + y) * 2 + core


def kernel(
    image, text, text_in, log_scale, bias,
    image_grad, text_grad, head_grad,
    raw, inv, low, acc, far, near, grad, tin_t, tin_p, tg_p,
    hbuf, tail, xs, xr, red, zs, zr, ysum, yr, zg, hg, hout,
    in_sem, out_sem, leg_s, far_r, fwd_s, fwd_r, near_s, near_r,
    tin_s, tin_r, tg_s, tg_r, xs_s, xs_r, zs_s, zs_r, ys_s, ys_r,
    zg_s, zg_r, xg_s, xg_r, kg_s, kg_r,
):
    me = lax.axis_index("dp")
    core, chip = me % 2, me // 2
    y, z, x = chip % NY, (chip // NY) % NZ, chip // (NY * NZ)
    above, below = (chip + 1) % CHIPS, (chip + CHIPS - 1) % CHIPS
    other = 2 * chip + 1 - core
    giver = jnp.where(core == 0, 2 * below, 2 * above)
    to_up, to_down = 2 * above, 2 * below + 1
    x_peer = [at((x + j) % NX, z, y, core) for j in range(NX)]
    y_peer = [at(x, z, (y + j) % NY, core) for j in range(NY)]
    z_peer = [at(x, (z + j) % NZ, y, core) for j in range(NZ)]

    barrier = pltpu.get_barrier_semaphore()
    peers = [giver, giver + 1, other] + x_peer[1:] + y_peer[1:] + z_peer[1:]
    for peer in peers:
        pl.semaphore_signal(barrier, inc=1, device_id=(peer,), device_id_type=MESH)

    loads = [
        pltpu.make_async_copy(image, raw.at[0], in_sem.at[0]),
        pltpu.make_async_copy(text, raw.at[1], in_sem.at[1]),
        pltpu.make_async_copy(text_in, tin_t, in_sem.at[2]),
    ]
    for load in loads:
        load.start()

    scale = jnp.exp(jnp.full((8, 128), log_scale[0], F32))[0:1, 0:1]
    shift = jnp.full((8, 128), bias[0], F32)[0:1, 0:1]

    def normalize(side):
        def body(n, _):
            rows = pl.ds(pl.multiple_of(n * 16, 16), 16)
            wide = raw[side, rows, :].astype(F32)
            inverse = lax.rsqrt(jnp.sum(wide * wide, axis=-1, keepdims=True) + EPS)
            low[side, rows, :] = (wide * inverse).astype(BF16)
            inv[side, rows, :] = jnp.broadcast_to(inverse, (16, 128))
            return 0

        lax.fori_loop(0, ROWS // 16, body, 0, unroll=2)

    def part(n):
        return pl.ds(pl.multiple_of(n * CH, CH), CH)

    passed, kept = 1 - core, core

    def leg(side, up, n):
        return remote(
            low.at[side, part(n)], far.at[side, core, n],
            leg_s.at[side, up, n], far_r.at[side, core, n], to_up if up else to_down,
        )

    def arrived(side, slot, n):
        return remote(
            low.at[side, part(n)], far.at[side, slot, n],
            leg_s.at[side, 0, n], far_r.at[side, slot, n], to_up,
        )

    def own_over(side, n):
        return remote(
            low.at[side, part(n)], near.at[side, 0, n],
            near_s.at[side, n], near_r.at[side, n], other,
        )

    def pass_on(side, n):
        return remote(
            far.at[side, passed, n], near.at[side, 1, n],
            fwd_s.at[side, n], fwd_r.at[side, n], other,
        )

    def send_side(side):
        for n in range(NCH):
            leg(side, 0, n).start()
            leg(side, 1, n).start()
            own_over(side, n).start()

    def gate(left, right):
        dots = lax.dot_general(left, right, (((1,), (1,)), ((), ())), preferred_element_type=F32)
        return jax.nn.sigmoid(scale * dots + shift)

    def own_tile(side):
        rest = low[1 - side]
        mine = low[side]
        tile = gate(rest, mine)
        row = lax.broadcasted_iota(jnp.int32, (ROWS, ROWS), 0)
        col = lax.broadcasted_iota(jnp.int32, (ROWS, ROWS), 1)
        tile = (tile - jnp.where(row == col, 1.0, 0.0)).astype(BF16)
        acc[side] = jnp.dot(tile, mine, preferred_element_type=F32)

    def add_rows(side, rows):
        tile = gate(low[1 - side], rows).astype(BF16)
        acc[side] += jnp.dot(tile, rows, preferred_element_type=F32)

    def add_near(side):
        def body(n, _):
            own_over(side, n).wait_recv()
            add_rows(side, near[side, 0, n])
            return 0

        lax.fori_loop(0, NCH, body, 0)

    def add_far(side, n):
        arrived(side, passed, n).wait_recv()
        pass_on(side, n).start()
        add_rows(side, far[side, passed, n])
        arrived(side, kept, n).wait_recv()
        add_rows(side, far[side, kept, n])
        pass_on(side, n).wait_recv()
        add_rows(side, near[side, 1, n])

    def finish(side, n):
        for part_of in range(CH // 16):
            rows = pl.ds(pl.multiple_of(n * CH + part_of * 16, 16), 16)
            inverse = inv[1 - side, rows, 0:1]
            total = scale * acc[side, rows, :]
            unit = raw[1 - side, rows, :].astype(F32) * inverse
            along = jnp.sum(unit * total, axis=-1, keepdims=True)
            grad[side, rows, :] = ((total - unit * along) * inverse).astype(BF16)

    def out_copy(side, n):
        dst = (text_grad, image_grad)[side]
        return pltpu.make_async_copy(grad.at[side, part(n)], dst.at[part(n)], out_sem.at[side, n])

    loads[0].wait()
    normalize(0)
    pl.semaphore_wait(barrier, len(peers))
    send_side(0)
    loads[1].wait()
    normalize(1)
    send_side(1)
    own_tile(0)
    loads[2].wait()
    tin_copy = remote(
        tin_t.at[pl.ds(pl.multiple_of(HALF * (1 - core), HALF), HALF)], tin_p,
        tin_s.at[0], tin_r.at[0], other,
    )
    tin_copy.start()
    own_tile(1)
    add_near(0)
    add_near(1)

    def image_step(n, _):
        add_far(0, n)
        return 0

    lax.fori_loop(0, NCH, image_step, 0)

    def tg_copy(n):
        return remote(
            grad.at[0, part(n), pl.ds(0, WIDE)], tg_p.at[part(n)], tg_s.at[n], tg_r.at[n], other,
        )

    def finish_text(n, _):
        finish(0, n)
        tg_copy(n).start()
        out_copy(0, n).start()
        return 0

    lax.fori_loop(0, NCH, finish_text, 0)
    half = pl.ds(pl.multiple_of(HALF * core, HALF), HALF)
    hbuf[...] = jnp.dot(tin_t[half, :], grad[0, :, 0:WIDE], preferred_element_type=F32)
    tin_copy.wait_recv()
    for n in range(NCH):
        tg_copy(n).wait_recv()
    hbuf[...] += jnp.dot(tin_p[...], tg_p[...], preferred_element_type=F32)

    tail[0:144] = jnp.concatenate([hbuf[0:144, 512:576], hbuf[144:288, 512:576]], axis=1)
    tail[144:192] = jnp.zeros((48, 128), F32)
    for q in range(NX):
        xs[q, 0:HALF] = hbuf[:, 128 * q : 128 * q + 128].astype(BF16)
        xs[q, HALF:PIECE] = tail[48 * q : 48 * q + 48].astype(BF16)
    x_copy = [
        remote(xs.at[(x + j) % NX], xr.at[j - 1], xs_s.at[j - 1], xs_r.at[j - 1], x_peer[j])
        for j in range(1, NX)
    ]
    for copy in x_copy:
        copy.start()
    red[0:HALF] = hbuf[:, pl.ds(pl.multiple_of(128 * x, 128), 128)]
    red[HALF:PIECE] = tail[pl.ds(pl.multiple_of(48 * x, 16), 48)]
    red[PIECE:PADDED] = jnp.zeros((PADDED - PIECE, 128), F32)

    add_far(1, 0)

    for j in range(1, NX):
        x_copy[j - 1].wait_recv()
        red[0:PIECE] += xr[j - 1].astype(F32)
    zs[...] = red[...].astype(BF16)

    def share(pos):
        return (pos * OWNERS + NZ - 1) // NZ

    def owns(pos):
        return (share(pos) * NZ) // OWNERS == pos

    def rows_of(pos):
        return pl.ds(pl.multiple_of(ZROWS * share(pos), ZROWS), ZROWS)

    mine = owns(z)
    z_at = [(z + j) % NZ for j in range(NZ)]

    def z_copy(j):
        return remote(zs.at[rows_of(z_at[j])], zr.at[j - 1], zs_s.at[j - 1], zs_r.at[j - 1], z_peer[j])

    far_first = sorted(range(1, NZ), key=lambda j: -min(j, NZ - j))
    for j in far_first:
        @pl.when(owns(z_at[j]))
        def _():
            z_copy(j).start()

    def y_copy(j):
        return remote(ysum, yr.at[y], ys_s.at[j - 1], ys_r.at[j - 1], y_peer[j])

    def zg_copy(j):
        return remote(zg.at[rows_of(z)], zg.at[rows_of(z)], zg_s.at[j - 1], zg_r.at[j - 1], z_peer[j])

    @pl.when(mine)
    def _():
        total = red[rows_of(z), :]
        for j in range(1, NZ):
            remote(zs.at[0:ZROWS], zr.at[j - 1], zs_s.at[j - 1], zs_r.at[j - 1], z_peer[j]).wait_recv()
            total += zr[j - 1].astype(F32)
        ysum[...] = total
        for j in range(1, NY):
            y_copy(j).start()

    add_far(1, 1)

    @pl.when(mine)
    def _():
        yr[y] = ysum[...]
        for j in range(1, NY):
            y_copy(j).wait_recv()
        total = (yr[0] + yr[1]) + (yr[2] + yr[3])
        zg[rows_of(z), :] = total.astype(BF16)
        for j in far_first:
            zg_copy(j).start()

    add_far(1, 2)

    for j in range(1, NZ):
        source = (z - j + NZ) % NZ

        @pl.when(owns(source))
        def _():
            remote(
                zg.at[rows_of(source)], zg.at[rows_of(source)], zg_s.at[j - 1], zg_r.at[j - 1], z_peer[j]
            ).wait_recv()

    def xg_copy(j):
        return remote(zg.at[0:PIECE], hg.at[core, x], xg_s.at[j - 1], xg_r.at[j - 1], x_peer[j])

    def kg_copy(j):
        slot = hg.at[core, (x + j) % NX]
        return remote(slot, slot, kg_s.at[j], kg_r.at[j], other)

    for j in range(1, NX):
        xg_copy(j).start()
    hg[core, x] = zg[0:PIECE]
    kg_copy(0).start()

    add_far(1, 3)

    for j in range(1, NX):
        source = (x - j + NX) % NX
        remote(zg.at[0:PIECE], hg.at[core, source], xg_s.at[j - 1], xg_r.at[j - 1], x_peer[j]).wait_recv()
        kg_copy(NX - j).start()

    def finish_image(n, _):
        finish(1, n)
        out_copy(1, n).start()
        return 0

    lax.fori_loop(0, NCH, finish_image, 0)

    for j in range(NX):
        slot = hg.at[1 - core, (x + j) % NX]
        remote(slot, slot, kg_s.at[j], kg_r.at[j], other).wait_recv()
    for k in range(2):
        for q in range(NX):
            hout[HALF * k : HALF * k + HALF, 128 * q : 128 * q + 128] = hg[k, q, 0:HALF]
        for q in range(NX - 1):
            last = hg[k, q, HALF:PIECE]
            for h in range(2):
                first = HALF * k + 144 * h + 48 * q
                hout[first : first + 48, 512:576] = last[:, 64 * h : 64 * h + 64]
    head_copy = pltpu.make_async_copy(hout, head_grad, out_sem.at[2, 0])
    head_copy.start()

    for side in range(2):
        for n in range(NCH):
            leg(side, 0, n).wait_send()
            leg(side, 1, n).wait_send()
            own_over(side, n).wait_send()
            pass_on(side, n).wait_send()
    tin_copy.wait_send()
    for n in range(NCH):
        tg_copy(n).wait_send()
    for j in range(1, NX):
        x_copy[j - 1].wait_send()
        xg_copy(j).wait_send()
    for j in range(NX):
        kg_copy(j).wait_send()
    for j in range(1, NZ):
        @pl.when(owns(z_at[j]))
        def _():
            z_copy(j).wait_send()

    @pl.when(mine)
    def _():
        for j in range(1, NY):
            y_copy(j).wait_send()
        for j in range(1, NZ):
            zg_copy(j).wait_send()

    for side in range(2):
        for n in range(NCH):
            out_copy(side, n).wait()
    head_copy.wait()


def per_device(image, text, text_in, log_scale, bias):
    dma = pltpu.SemaphoreType.DMA
    vmem = pltpu.VMEM
    anywhere = pl.BlockSpec(memory_space=pl.ANY)
    scalars = pl.BlockSpec(memory_space=pltpu.SMEM)
    return pl.pallas_call(
        kernel,
        out_shape=(
            jax.ShapeDtypeStruct((ROWS, D), BF16),
            jax.ShapeDtypeStruct((ROWS, D), BF16),
            jax.ShapeDtypeStruct((HIN, HOUT), BF16),
        ),
        in_specs=[anywhere, anywhere, anywhere, scalars, scalars],
        out_specs=(anywhere, anywhere, anywhere),
        scratch_shapes=[
            vmem((2, ROWS, D), BF16),
            vmem((2, ROWS, 128), F32),
            vmem((2, ROWS, D), BF16),
            vmem((2, ROWS, D), F32),
            vmem((2, 2, NCH, CH, D), BF16),
            vmem((2, 2, NCH, CH, D), BF16),
            vmem((2, ROWS, D), BF16),
            vmem((HIN, ROWS), BF16),
            vmem((HALF, ROWS), BF16),
            vmem((ROWS, WIDE), BF16),
            vmem((HALF, WIDE), F32),
            vmem((192, 128), F32),
            vmem((NX, PIECE, 128), BF16),
            vmem((NX - 1, PIECE, 128), BF16),
            vmem((PADDED, 128), F32),
            vmem((PADDED, 128), BF16),
            vmem((NZ - 1, ZROWS, 128), BF16),
            vmem((ZROWS, 128), F32),
            vmem((NY, ZROWS, 128), F32),
            vmem((PADDED, 128), BF16),
            vmem((2, NX, PIECE, 128), BF16),
            vmem((HIN, HOUT), BF16),
            dma((3,)), dma((3, NCH)),
            dma((2, 2, NCH)), dma((2, 2, NCH)),
            dma((2, NCH)), dma((2, NCH)), dma((2, NCH)), dma((2, NCH)),
            dma((1,)), dma((1,)), dma((NCH,)), dma((NCH,)),
            dma((NX - 1,)), dma((NX - 1,)), dma((NZ - 1,)), dma((NZ - 1,)),
            dma((NY - 1,)), dma((NY - 1,)), dma((NZ - 1,)), dma((NZ - 1,)),
            dma((NX - 1,)), dma((NX - 1,)), dma((NX,)), dma((NX,)),
        ],
        compiler_params=pltpu.CompilerParams(
            collective_id=1, has_side_effects=True, vmem_limit_bytes=60 * 2**20
        ),
        cost_estimate=pl.CostEstimate(flops=7 * 10**9, bytes_accessed=5 * 10**6, transcendentals=2 * 10**6),
        name="band",
    )(image, text, text_in.T, log_scale, bias)


def solution(mesh):
    placed = (P("dp", None), P("dp", None), P("dp", None), P(), P())
    return jax.shard_map(
        per_device,
        mesh=mesh,
        in_specs=placed,
        out_specs=(P("dp", None), P("dp", None), P()),
        check_vma=False,
    )
```

```python
import functools

import jax
import jax.numpy as jnp
from jax import lax
from jax.experimental import pallas as pl
from jax.experimental.pallas import tpu as pltpu
from jax.sharding import PartitionSpec as P

D = 1152
HIN = 576
HOUT = 576
ROWS = 384
EPS = 1e-06

NX, NZ, NY = 4, 16, 4
CHIPS = NX * NZ * NY
NCH = 4
CH = ROWS // NCH
HALF = HIN // 2
WIDE = 640
PIECE = 336
OWNERS = 11
ZROWS = 32
PADDED = OWNERS * ZROWS
CUT = 192
PARTS = ((0, CUT), (CUT, PIECE - CUT))

SPLIT = 2

MESH = pl.DeviceIdType.MESH
BF16 = jnp.bfloat16
F32 = jnp.float32


def remote(src, dst, send, recv, device):
    return pltpu.make_async_remote_copy(
        src_ref=src, dst_ref=dst, send_sem=send, recv_sem=recv,
        device_id=(device,), device_id_type=MESH,
    )


def at(x, z, y, core):
    return ((x * NZ + z) * NY + y) * 2 + core


def kernel(
    image, text, text_in, log_scale, bias,
    image_grad, text_grad, head_grad,
    raw, inv, low, acc, far, near, grad, tin_t, tin_p, tg_p,
    hbuf, tail, xs, xr, red, zs, zr, ysum, yr, zg, hg, hout,
    in_sem, out_sem, leg_s, far_r, fwd_s, fwd_r, near_s, near_r,
    tin_s, tin_r, tg_s, tg_r, xs_s, xs_r, zs_s, zs_r, ys_s, ys_r,
    zg_s, zg_r, xg_s, xg_r, kg_s, kg_r,
):
    me = lax.axis_index("dp")
    core, chip = me % 2, me // 2
    y, z, x = chip % NY, (chip // NY) % NZ, chip // (NY * NZ)
    above, below = (chip + 1) % CHIPS, (chip + CHIPS - 1) % CHIPS
    other = 2 * chip + 1 - core
    giver = jnp.where(core == 0, 2 * below, 2 * above)
    to_up, to_down = 2 * above, 2 * below + 1
    x_peer = [at((x + j) % NX, z, y, core) for j in range(NX)]
    y_peer = [at(x, z, (y + j) % NY, core) for j in range(NY)]
    z_peer = [at(x, (z + j) % NZ, y, core) for j in range(NZ)]

    barrier = pltpu.get_barrier_semaphore()
    peers = [giver, giver + 1, other] + x_peer[1:] + y_peer[1:] + z_peer[1:]
    for peer in peers:
        pl.semaphore_signal(barrier, inc=1, device_id=(peer,), device_id_type=MESH)

    loads = [
        pltpu.make_async_copy(image, raw.at[0], in_sem.at[0]),
        pltpu.make_async_copy(text, raw.at[1], in_sem.at[1]),
        pltpu.make_async_copy(text_in, tin_t, in_sem.at[2]),
    ]
    for load in loads:
        load.start()

    scale = jnp.exp(jnp.full((8, 128), log_scale[0], F32))[0:1, 0:1]
    shift = jnp.full((8, 128), bias[0], F32)[0:1, 0:1]

    def normalize(side):
        def body(n, _):
            rows = pl.ds(pl.multiple_of(n * 16, 16), 16)
            wide = raw[side, rows, :].astype(F32)
            inverse = lax.rsqrt(jnp.sum(wide * wide, axis=-1, keepdims=True) + EPS)
            low[side, rows, :] = (wide * inverse).astype(BF16)
            inv[side, rows, :] = jnp.broadcast_to(inverse, (16, 128))
            return 0

        lax.fori_loop(0, ROWS // 16, body, 0, unroll=2)

    def part(n):
        return pl.ds(pl.multiple_of(n * CH, CH), CH)

    passed, kept = 1 - core, core

    def leg(side, up, n):
        return remote(
            low.at[side, part(n)], far.at[side, core, n],
            leg_s.at[side, up, n], far_r.at[side, core, n], to_up if up else to_down,
        )

    def arrived(side, slot, n):
        return remote(
            low.at[side, part(n)], far.at[side, slot, n],
            leg_s.at[side, 0, n], far_r.at[side, slot, n], to_up,
        )

    def own_over(side, n):
        return remote(
            low.at[side, part(n)], near.at[side, 0, n],
            near_s.at[side, n], near_r.at[side, n], other,
        )

    def pass_on(side, n):
        return remote(
            far.at[side, passed, n], near.at[side, 1, n],
            fwd_s.at[side, n], fwd_r.at[side, n], other,
        )

    def send_side(side):
        for n in range(NCH):
            leg(side, 0, n).start()
            leg(side, 1, n).start()
            own_over(side, n).start()

    def gate(left, right):
        dots = lax.dot_general(left, right, (((1,), (1,)), ((), ())), preferred_element_type=F32)
        return jax.nn.sigmoid(scale * dots + shift)

    def own_tile(side):
        rest = low[1 - side]
        mine = low[side]
        tile = gate(rest, mine)
        row = lax.broadcasted_iota(jnp.int32, (ROWS, ROWS), 0)
        col = lax.broadcasted_iota(jnp.int32, (ROWS, ROWS), 1)
        tile = (tile - jnp.where(row == col, 1.0, 0.0)).astype(BF16)
        acc[side] = jnp.dot(tile, mine, preferred_element_type=F32)

    def add_rows(side, rows):
        tile = gate(low[1 - side], rows).astype(BF16)
        acc[side] += jnp.dot(tile, rows, preferred_element_type=F32)

    def add_near(side):
        def body(n, _):
            own_over(side, n).wait_recv()
            add_rows(side, near[side, 0, n])
            return 0

        lax.fori_loop(0, NCH, body, 0)

    def add_far(side, n):
        arrived(side, passed, n).wait_recv()
        pass_on(side, n).start()
        add_rows(side, far[side, passed, n])
        arrived(side, kept, n).wait_recv()
        add_rows(side, far[side, kept, n])
        pass_on(side, n).wait_recv()
        add_rows(side, near[side, 1, n])

    def finish(side, n):
        for part_of in range(CH // 16):
            rows = pl.ds(pl.multiple_of(n * CH + part_of * 16, 16), 16)
            inverse = inv[1 - side, rows, 0:1]
            total = scale * acc[side, rows, :]
            unit = raw[1 - side, rows, :].astype(F32) * inverse
            along = jnp.sum(unit * total, axis=-1, keepdims=True)
            grad[side, rows, :] = ((total - unit * along) * inverse).astype(BF16)

    def out_copy(side, n):
        dst = (text_grad, image_grad)[side]
        return pltpu.make_async_copy(grad.at[side, part(n)], dst.at[part(n)], out_sem.at[side, n])

    loads[0].wait()
    normalize(0)
    pl.semaphore_wait(barrier, len(peers))
    send_side(0)
    loads[1].wait()
    normalize(1)
    send_side(1)
    own_tile(0)
    loads[2].wait()
    tin_copy = remote(
        tin_t.at[pl.ds(pl.multiple_of(HALF * (1 - core), HALF), HALF)], tin_p,
        tin_s.at[0], tin_r.at[0], other,
    )
    tin_copy.start()
    own_tile(1)
    add_near(0)
    add_near(1)

    def image_step(n, _):
        add_far(0, n)
        return 0

    lax.fori_loop(0, NCH, image_step, 0)

    def tg_copy(n):
        return remote(
            grad.at[0, part(n), pl.ds(0, WIDE)], tg_p.at[part(n)], tg_s.at[n], tg_r.at[n], other,
        )

    def finish_text(n, _):
        finish(0, n)
        tg_copy(n).start()
        out_copy(0, n).start()
        return 0

    lax.fori_loop(0, NCH, finish_text, 0)
    half = pl.ds(pl.multiple_of(HALF * core, HALF), HALF)
    hbuf[...] = jnp.dot(tin_t[half, :], grad[0, :, 0:WIDE], preferred_element_type=F32)
    tin_copy.wait_recv()
    for n in range(NCH):
        tg_copy(n).wait_recv()
    hbuf[...] += jnp.dot(tin_p[...], tg_p[...], preferred_element_type=F32)

    tail[0:144] = jnp.concatenate([hbuf[0:144, 512:576], hbuf[144:288, 512:576]], axis=1)
    tail[144:192] = jnp.zeros((48, 128), F32)
    for q in range(NX):
        xs[q, 0:HALF] = hbuf[:, 128 * q : 128 * q + 128].astype(BF16)
        xs[q, HALF:PIECE] = tail[48 * q : 48 * q + 48].astype(BF16)
    def x_copy(h, j):
        rows = pl.ds(*PARTS[h])
        return remote(
            xs.at[(x + j) % NX, rows], xr.at[j - 1, rows], xs_s.at[h, j - 1], xs_r.at[h, j - 1], x_peer[j]
        )

    for h in range(2):
        for j in range(1, NX):
            x_copy(h, j).start()
    red[0:HALF] = hbuf[:, pl.ds(pl.multiple_of(128 * x, 128), 128)]
    red[HALF:PIECE] = tail[pl.ds(pl.multiple_of(48 * x, 16), 48)]
    red[PIECE:PADDED] = jnp.zeros((PADDED - PIECE, 128), F32)
    zs[PIECE:PADDED] = jnp.zeros((PADDED - PIECE, 128), BF16)

    add_far(1, 0)

    def share(pos):
        return (pos * OWNERS + NZ - 1) // NZ

    def owns(pos):
        return (share(pos) * NZ) // OWNERS == pos

    def owns_in(h, pos):
        return jnp.logical_and(owns(pos), share(pos) % 2 == h)

    def rows_of(pos):
        first = CUT * (share(pos) % 2) + ZROWS * (share(pos) // 2)
        return pl.ds(pl.multiple_of(first, ZROWS), ZROWS)

    mine = owns(z)
    z_at = [(z + j) % NZ for j in range(NZ)]

    def z_copy(j):
        return remote(zs.at[rows_of(z_at[j])], zr.at[j - 1], zs_s.at[j - 1], zs_r.at[j - 1], z_peer[j])

    far_first = sorted(range(1, NZ), key=lambda j: -min(j, NZ - j))
    for h in range(2):
        rows = pl.ds(*PARTS[h])
        for j in range(1, NX):
            x_copy(h, j).wait_recv()
            red[rows] += xr[j - 1, rows].astype(F32)
        zs[rows] = red[rows].astype(BF16)
        for j in far_first:
            @pl.when(owns_in(h, z_at[j]))
            def _():
                z_copy(j).start()

    def y_copy(j):
        return remote(ysum, yr.at[y], ys_s.at[j - 1], ys_r.at[j - 1], y_peer[j])

    def zg_copy(j):
        return remote(zg.at[rows_of(z)], zg.at[rows_of(z)], zg_s.at[j - 1], zg_r.at[j - 1], z_peer[j])

    @pl.when(mine)
    def _():
        total = red[rows_of(z), :]
        for j in range(1, NZ):
            remote(zs.at[0:ZROWS], zr.at[j - 1], zs_s.at[j - 1], zs_r.at[j - 1], z_peer[j]).wait_recv()
            total += zr[j - 1].astype(F32)
        ysum[...] = total
        for j in range(1, NY):
            y_copy(j).start()

    add_far(1, 1)

    @pl.when(mine)
    def _():
        yr[y] = ysum[...]
        for j in range(1, NY):
            y_copy(j).wait_recv()
        total = (yr[0] + yr[1]) + (yr[2] + yr[3])
        zg[rows_of(z), :] = total.astype(BF16)
        for j in far_first:
            zg_copy(j).start()

    add_far(1, 2)

    def xg_copy(h, j):
        rows = pl.ds(*PARTS[h])
        return remote(
            zg.at[rows], hg.at[core, x, rows], xg_s.at[h, j - 1], xg_r.at[h, j - 1], x_peer[j]
        )

    def xg_wait(h, j):
        rows = pl.ds(*PARTS[h])
        source = (x - j + NX) % NX
        remote(
            zg.at[rows], hg.at[core, source, rows], xg_s.at[h, j - 1], xg_r.at[h, j - 1], x_peer[j]
        ).wait_recv()

    def kg_copy(h, j, side):
        slot = hg.at[side, (x + j) % NX, pl.ds(*PARTS[h])]
        return remote(slot, slot, kg_s.at[h, j], kg_r.at[h, j], other)

    for h in range(2):
        for j in range(1, NZ):
            source = (z - j + NZ) % NZ

            @pl.when(owns_in(h, source))
            def _():
                remote(
                    zg.at[rows_of(source)], zg.at[rows_of(source)],
                    zg_s.at[j - 1], zg_r.at[j - 1], z_peer[j],
                ).wait_recv()

        for j in range(1, NX):
            xg_copy(h, j).start()
        rows = pl.ds(*PARTS[h])
        hg[core, x, rows] = zg[rows]
        kg_copy(h, 0, core).start()

    add_far(1, 3)

    for h in range(2):
        for j in range(1, NX):
            xg_wait(h, j)
            kg_copy(h, NX - j, core).start()

    def finish_image(n, _):
        finish(1, n)
        out_copy(1, n).start()
        return 0

    lax.fori_loop(0, NCH, finish_image, 0)

    for h in range(2):
        for j in range(NX):
            kg_copy(h, j, 1 - core).wait_recv()
    for k in range(2):
        for q in range(NX):
            hout[HALF * k : HALF * k + HALF, 128 * q : 128 * q + 128] = hg[k, q, 0:HALF]
        for q in range(NX - 1):
            last = hg[k, q, HALF:PIECE]
            for h in range(2):
                first = HALF * k + 144 * h + 48 * q
                hout[first : first + 48, 512:576] = last[:, 64 * h : 64 * h + 64]
    head_copy = pltpu.make_async_copy(hout, head_grad, out_sem.at[2, 0])
    head_copy.start()

    for side in range(2):
        for n in range(NCH):
            leg(side, 0, n).wait_send()
            leg(side, 1, n).wait_send()
            own_over(side, n).wait_send()
            pass_on(side, n).wait_send()
    tin_copy.wait_send()
    for n in range(NCH):
        tg_copy(n).wait_send()
    for h in range(2):
        for j in range(1, NX):
            x_copy(h, j).wait_send()
            xg_copy(h, j).wait_send()
        for j in range(NX):
            kg_copy(h, j, core).wait_send()
    for j in range(1, NZ):
        @pl.when(owns(z_at[j]))
        def _():
            z_copy(j).wait_send()

    @pl.when(mine)
    def _():
        for j in range(1, NY):
            y_copy(j).wait_send()
        for j in range(1, NZ):
            zg_copy(j).wait_send()

    for side in range(2):
        for n in range(NCH):
            out_copy(side, n).wait()
    head_copy.wait()


def hand_over(*refs):
    sources, results, held, in_sems, out_sems = refs[:3], refs[3:6], refs[6:9], refs[9], refs[10]
    reads, writes = [], []
    for i, (src, dst, mid) in enumerate(zip(sources, results, held)):
        rows = src.shape[0] // SPLIT
        for n in range(SPLIT):
            part = pl.ds(n * rows, rows)
            reads.append(pltpu.make_async_copy(src.at[part], mid.at[part], in_sems.at[i, n]))
            writes.append(pltpu.make_async_copy(mid.at[part], dst.at[part], out_sems.at[i, n]))
    for read in reads:
        read.start()
    for read, write in zip(reads, writes):
        read.wait()
        write.start()
    for write in writes:
        write.wait()


def per_device(image, text, text_in, log_scale, bias):
    dma = pltpu.SemaphoreType.DMA
    vmem = pltpu.VMEM
    anywhere = pl.BlockSpec(memory_space=pl.ANY)
    scalars = pl.BlockSpec(memory_space=pltpu.SMEM)
    grads = pl.pallas_call(
        kernel,
        out_shape=(
            jax.ShapeDtypeStruct((ROWS, D), BF16),
            jax.ShapeDtypeStruct((ROWS, D), BF16),
            jax.ShapeDtypeStruct((HIN, HOUT), BF16),
        ),
        in_specs=[anywhere, anywhere, anywhere, scalars, scalars],
        out_specs=(anywhere, anywhere, anywhere),
        scratch_shapes=[
            vmem((2, ROWS, D), BF16),
            vmem((2, ROWS, 128), F32),
            vmem((2, ROWS, D), BF16),
            vmem((2, ROWS, D), F32),
            vmem((2, 2, NCH, CH, D), BF16),
            vmem((2, 2, NCH, CH, D), BF16),
            vmem((2, ROWS, D), BF16),
            vmem((HIN, ROWS), BF16),
            vmem((HALF, ROWS), BF16),
            vmem((ROWS, WIDE), BF16),
            vmem((HALF, WIDE), F32),
            vmem((192, 128), F32),
            vmem((NX, PIECE, 128), BF16),
            vmem((NX - 1, PIECE, 128), BF16),
            vmem((PADDED, 128), F32),
            vmem((PADDED, 128), BF16),
            vmem((NZ - 1, ZROWS, 128), BF16),
            vmem((ZROWS, 128), F32),
            vmem((NY, ZROWS, 128), F32),
            vmem((PADDED, 128), BF16),
            vmem((2, NX, PIECE, 128), BF16),
            vmem((HIN, HOUT), BF16),
            dma((3,)), dma((3, NCH)),
            dma((2, 2, NCH)), dma((2, 2, NCH)),
            dma((2, NCH)), dma((2, NCH)), dma((2, NCH)), dma((2, NCH)),
            dma((1,)), dma((1,)), dma((NCH,)), dma((NCH,)),
            dma((2, NX - 1)), dma((2, NX - 1)), dma((NZ - 1,)), dma((NZ - 1,)),
            dma((NY - 1,)), dma((NY - 1,)), dma((NZ - 1,)), dma((NZ - 1,)),
            dma((2, NX - 1)), dma((2, NX - 1)), dma((2, NX)), dma((2, NX)),
        ],
        compiler_params=pltpu.CompilerParams(
            collective_id=1, has_side_effects=True, vmem_limit_bytes=60 * 2**20
        ),
        cost_estimate=pl.CostEstimate(flops=7 * 10**9, bytes_accessed=5 * 10**6, transcendentals=2 * 10**6),
        name="band",
    )(image, text, text_in.T, log_scale, bias)
    return pl.pallas_call(
        hand_over,
        out_shape=tuple(jax.ShapeDtypeStruct(g.shape, g.dtype) for g in grads),
        in_specs=[anywhere] * 3,
        out_specs=(anywhere,) * 3,
        scratch_shapes=[vmem(g.shape, g.dtype) for g in grads] + [dma((3, SPLIT)), dma((3, SPLIT))],
        cost_estimate=pl.CostEstimate(flops=0, bytes_accessed=5 * 10**6, transcendentals=0),
        name="hand_over",
    )(*grads)


def solution(mesh):
    placed = (P("dp", None), P("dp", None), P("dp", None), P(), P())
    return jax.shard_map(
        per_device,
        mesh=mesh,
        in_specs=placed,
        out_specs=(P("dp", None), P("dp", None), P()),
        check_vma=False,
    )
```

```python
import functools

import jax
import jax.numpy as jnp
from jax import lax
from jax.experimental import pallas as pl
from jax.experimental.pallas import tpu as pltpu
from jax.sharding import PartitionSpec as P

D = 1152
HIN = 576
HOUT = 576
ROWS = 384
EPS = 1e-06

NX, NZ, NY = 4, 16, 4
CHIPS = NX * NZ * NY
NCH = 4
CH = ROWS // NCH
HALF = HIN // 2
WIDE = 640
PIECE = 336
OWNERS = 11
ZROWS = 32
PADDED = OWNERS * ZROWS
CUT = 192
PARTS = ((0, CUT), (CUT, PIECE - CUT))

SPLIT = 2

MESH = pl.DeviceIdType.MESH
BF16 = jnp.bfloat16
F32 = jnp.float32


def remote(src, dst, send, recv, device):
    return pltpu.make_async_remote_copy(
        src_ref=src, dst_ref=dst, send_sem=send, recv_sem=recv,
        device_id=(device,), device_id_type=MESH,
    )


def at(x, z, y, core):
    return ((x * NZ + z) * NY + y) * 2 + core


def kernel(
    image, text, text_in, log_scale, bias,
    image_grad, text_grad, head_grad,
    raw, inv, low, acc, far, near, grad, tin_t, tin_p, tg_p,
    hbuf, tail, xs, xr, red, zs, zr, ysum, yr, zg, hg, hout,
    in_sem, out_sem, leg_s, far_r, fwd_s, fwd_r, near_s, near_r,
    tin_s, tin_r, tg_s, tg_r, xs_s, xs_r, zs_s, zs_r, ys_s, ys_r,
    zg_s, zg_r, xg_s, xg_r, kg_s, kg_r,
):
    me = lax.axis_index("dp")
    core, chip = me % 2, me // 2
    y, z, x = chip % NY, (chip // NY) % NZ, chip // (NY * NZ)
    above, below = (chip + 1) % CHIPS, (chip + CHIPS - 1) % CHIPS
    other = 2 * chip + 1 - core
    giver = jnp.where(core == 0, 2 * below, 2 * above)
    to_up, to_down = 2 * above, 2 * below + 1
    x_peer = [at((x + j) % NX, z, y, core) for j in range(NX)]
    y_peer = [at(x, z, (y + j) % NY, core) for j in range(NY)]
    z_peer = [at(x, (z + j) % NZ, y, core) for j in range(NZ)]

    barrier = pltpu.get_barrier_semaphore()
    peers = [giver, giver + 1, other] + x_peer[1:] + y_peer[1:] + z_peer[1:]
    for peer in peers:
        pl.semaphore_signal(barrier, inc=1, device_id=(peer,), device_id_type=MESH)

    loads = [
        pltpu.make_async_copy(image, raw.at[0], in_sem.at[0]),
        pltpu.make_async_copy(text, raw.at[1], in_sem.at[1]),
        pltpu.make_async_copy(text_in, tin_t, in_sem.at[2]),
    ]
    for load in loads:
        load.start()

    scale = jnp.exp(jnp.full((8, 128), log_scale[0], F32))[0:1, 0:1]
    shift = jnp.full((8, 128), bias[0], F32)[0:1, 0:1]

    def normalize(side):
        def body(n, _):
            rows = pl.ds(pl.multiple_of(n * 16, 16), 16)
            wide = raw[side, rows, :].astype(F32)
            inverse = lax.rsqrt(jnp.sum(wide * wide, axis=-1, keepdims=True) + EPS)
            low[side, rows, :] = (wide * inverse).astype(BF16)
            inv[side, rows, :] = jnp.broadcast_to(inverse, (16, 128))
            return 0

        lax.fori_loop(0, ROWS // 16, body, 0, unroll=2)

    def part(n):
        return pl.ds(pl.multiple_of(n * CH, CH), CH)

    passed, kept = 1 - core, core

    def leg(side, up, n):
        return remote(
            low.at[side, part(n)], far.at[side, core, n],
            leg_s.at[side, up, n], far_r.at[side, core, n], to_up if up else to_down,
        )

    def arrived(side, slot, n):
        return remote(
            low.at[side, part(n)], far.at[side, slot, n],
            leg_s.at[side, 0, n], far_r.at[side, slot, n], to_up,
        )

    def own_over(side, n):
        return remote(
            low.at[side, part(n)], near.at[side, 0, n],
            near_s.at[side, n], near_r.at[side, n], other,
        )

    def pass_on(side, n):
        return remote(
            far.at[side, passed, n], near.at[side, 1, n],
            fwd_s.at[side, n], fwd_r.at[side, n], other,
        )

    def send_side(side):
        for n in range(NCH):
            leg(side, 0, n).start()
            leg(side, 1, n).start()
            own_over(side, n).start()

    def gate(left, right):
        dots = lax.dot_general(left, right, (((1,), (1,)), ((), ())), preferred_element_type=F32)
        return jax.nn.sigmoid(scale * dots + shift)

    def own_tile(side):
        rest = low[1 - side]
        mine = low[side]
        tile = gate(rest, mine)
        row = lax.broadcasted_iota(jnp.int32, (ROWS, ROWS), 0)
        col = lax.broadcasted_iota(jnp.int32, (ROWS, ROWS), 1)
        tile = (tile - jnp.where(row == col, 1.0, 0.0)).astype(BF16)
        acc[side] = jnp.dot(tile, mine, preferred_element_type=F32)

    def add_rows(side, rows):
        tile = gate(low[1 - side], rows).astype(BF16)
        acc[side] += jnp.dot(tile, rows, preferred_element_type=F32)

    def add_near(side):
        def body(n, _):
            own_over(side, n).wait_recv()
            add_rows(side, near[side, 0, n])
            return 0

        lax.fori_loop(0, NCH, body, 0)

    def add_far(side, n):
        arrived(side, passed, n).wait_recv()
        pass_on(side, n).start()
        add_rows(side, far[side, passed, n])
        arrived(side, kept, n).wait_recv()
        add_rows(side, far[side, kept, n])
        pass_on(side, n).wait_recv()
        add_rows(side, near[side, 1, n])

    def finish(side, n):
        for part_of in range(CH // 16):
            rows = pl.ds(pl.multiple_of(n * CH + part_of * 16, 16), 16)
            inverse = inv[1 - side, rows, 0:1]
            total = scale * acc[side, rows, :]
            unit = raw[1 - side, rows, :].astype(F32) * inverse
            along = jnp.sum(unit * total, axis=-1, keepdims=True)
            grad[side, rows, :] = ((total - unit * along) * inverse).astype(BF16)

    def out_copy(side, n):
        dst = (text_grad, image_grad)[side]
        return pltpu.make_async_copy(grad.at[side, part(n)], dst.at[part(n)], out_sem.at[side, n])

    loads[0].wait()
    normalize(0)
    pl.semaphore_wait(barrier, len(peers))
    send_side(0)
    loads[1].wait()
    normalize(1)
    send_side(1)
    own_tile(0)
    loads[2].wait()
    tin_copy = remote(
        tin_t.at[pl.ds(pl.multiple_of(HALF * (1 - core), HALF), HALF)], tin_p,
        tin_s.at[0], tin_r.at[0], other,
    )
    tin_copy.start()
    own_tile(1)
    add_near(0)
    add_near(1)

    def image_step(n, _):
        add_far(0, n)
        return 0

    lax.fori_loop(0, NCH, image_step, 0)

    def tg_copy(n):
        return remote(
            grad.at[0, part(n), pl.ds(0, WIDE)], tg_p.at[part(n)], tg_s.at[n], tg_r.at[n], other,
        )

    def finish_text(n, _):
        finish(0, n)
        tg_copy(n).start()
        out_copy(0, n).start()
        return 0

    lax.fori_loop(0, NCH, finish_text, 0)
    half = pl.ds(pl.multiple_of(HALF * core, HALF), HALF)
    hbuf[...] = jnp.dot(tin_t[half, :], grad[0, :, 0:WIDE], preferred_element_type=F32)
    tin_copy.wait_recv()
    for n in range(NCH):
        tg_copy(n).wait_recv()
    hbuf[...] += jnp.dot(tin_p[...], tg_p[...], preferred_element_type=F32)

    tail[0:144] = jnp.concatenate([hbuf[0:144, 512:576], hbuf[144:288, 512:576]], axis=1)
    tail[144:192] = jnp.zeros((48, 128), F32)
    for q in range(NX):
        xs[q, 0:HALF] = hbuf[:, 128 * q : 128 * q + 128].astype(BF16)
        xs[q, HALF:PIECE] = tail[48 * q : 48 * q + 48].astype(BF16)
    def x_copy(h, j):
        rows = pl.ds(*PARTS[h])
        return remote(
            xs.at[(x + j) % NX, rows], xr.at[j - 1, rows], xs_s.at[h, j - 1], xs_r.at[h, j - 1], x_peer[j]
        )

    for h in range(2):
        for j in range(1, NX):
            x_copy(h, j).start()
    red[0:HALF] = hbuf[:, pl.ds(pl.multiple_of(128 * x, 128), 128)]
    red[HALF:PIECE] = tail[pl.ds(pl.multiple_of(48 * x, 16), 48)]
    red[PIECE:PADDED] = jnp.zeros((PADDED - PIECE, 128), F32)
    zs[PIECE:PADDED] = jnp.zeros((PADDED - PIECE, 128), BF16)

    add_far(1, 0)

    def share(pos):
        return (pos * OWNERS + NZ - 1) // NZ

    def owns(pos):
        return (share(pos) * NZ) // OWNERS == pos

    def owns_in(h, pos):
        return jnp.logical_and(owns(pos), share(pos) % 2 == h)

    def rows_of(pos):
        first = CUT * (share(pos) % 2) + ZROWS * (share(pos) // 2)
        return pl.ds(pl.multiple_of(first, ZROWS), ZROWS)

    mine = owns(z)
    z_at = [(z + j) % NZ for j in range(NZ)]

    def z_copy(j):
        return remote(zs.at[rows_of(z_at[j])], zr.at[j - 1], zs_s.at[j - 1], zs_r.at[j - 1], z_peer[j])

    far_first = sorted(range(1, NZ), key=lambda j: -min(j, NZ - j))
    for h in range(2):
        rows = pl.ds(*PARTS[h])
        for j in range(1, NX):
            x_copy(h, j).wait_recv()
            red[rows] += xr[j - 1, rows].astype(F32)
        zs[rows] = red[rows].astype(BF16)
        for j in far_first:
            @pl.when(owns_in(h, z_at[j]))
            def _():
                z_copy(j).start()

    def y_copy(j):
        return remote(ysum, yr.at[y], ys_s.at[j - 1], ys_r.at[j - 1], y_peer[j])

    def zg_copy(j):
        return remote(zg.at[rows_of(z)], zg.at[rows_of(z)], zg_s.at[j - 1], zg_r.at[j - 1], z_peer[j])

    @pl.when(mine)
    def _():
        total = red[rows_of(z), :]
        for j in range(1, NZ):
            remote(zs.at[0:ZROWS], zr.at[j - 1], zs_s.at[j - 1], zs_r.at[j - 1], z_peer[j]).wait_recv()
            total += zr[j - 1].astype(F32)
        ysum[...] = total
        for j in range(1, NY):
            y_copy(j).start()

    add_far(1, 1)

    @pl.when(mine)
    def _():
        yr[y] = ysum[...]
        for j in range(1, NY):
            y_copy(j).wait_recv()
        total = (yr[0] + yr[1]) + (yr[2] + yr[3])
        zg[rows_of(z), :] = total.astype(BF16)
        for j in far_first:
            zg_copy(j).start()

    add_far(1, 2)

    def xg_copy(h, j):
        rows = pl.ds(*PARTS[h])
        return remote(
            zg.at[rows], hg.at[core, x, rows], xg_s.at[h, j - 1], xg_r.at[h, j - 1], x_peer[j]
        )

    def xg_wait(h, j):
        rows = pl.ds(*PARTS[h])
        source = (x - j + NX) % NX
        remote(
            zg.at[rows], hg.at[core, source, rows], xg_s.at[h, j - 1], xg_r.at[h, j - 1], x_peer[j]
        ).wait_recv()

    def kg_copy(h, j, side):
        slot = hg.at[side, (x + j) % NX, pl.ds(*PARTS[h])]
        return remote(slot, slot, kg_s.at[h, j], kg_r.at[h, j], other)

    for h in range(2):
        for j in range(1, NZ):
            source = (z - j + NZ) % NZ

            @pl.when(owns_in(h, source))
            def _():
                remote(
                    zg.at[rows_of(source)], zg.at[rows_of(source)],
                    zg_s.at[j - 1], zg_r.at[j - 1], z_peer[j],
                ).wait_recv()

        for j in range(1, NX):
            xg_copy(h, j).start()
        rows = pl.ds(*PARTS[h])
        hg[core, x, rows] = zg[rows]
        kg_copy(h, 0, core).start()

    add_far(1, 3)

    def finish_image(n, _):
        finish(1, n)
        out_copy(1, n).start()
        return 0

    lax.fori_loop(0, NCH, finish_image, 0)

    for h in range(2):
        for j in range(1, NX):
            xg_wait(h, j)
            kg_copy(h, NX - j, core).start()

    for h in range(2):
        for j in range(NX):
            kg_copy(h, j, 1 - core).wait_recv()
    for k in range(2):
        for q in range(NX):
            hout[HALF * k : HALF * k + HALF, 128 * q : 128 * q + 128] = hg[k, q, 0:HALF]
        for q in range(NX - 1):
            last = hg[k, q, HALF:PIECE]
            for h in range(2):
                first = HALF * k + 144 * h + 48 * q
                hout[first : first + 48, 512:576] = last[:, 64 * h : 64 * h + 64]
    head_copy = pltpu.make_async_copy(hout, head_grad, out_sem.at[2, 0])
    head_copy.start()

    for side in range(2):
        for n in range(NCH):
            leg(side, 0, n).wait_send()
            leg(side, 1, n).wait_send()
            own_over(side, n).wait_send()
            pass_on(side, n).wait_send()
    tin_copy.wait_send()
    for n in range(NCH):
        tg_copy(n).wait_send()
    for h in range(2):
        for j in range(1, NX):
            x_copy(h, j).wait_send()
            xg_copy(h, j).wait_send()
        for j in range(NX):
            kg_copy(h, j, core).wait_send()
    for j in range(1, NZ):
        @pl.when(owns(z_at[j]))
        def _():
            z_copy(j).wait_send()

    @pl.when(mine)
    def _():
        for j in range(1, NY):
            y_copy(j).wait_send()
        for j in range(1, NZ):
            zg_copy(j).wait_send()

    for side in range(2):
        for n in range(NCH):
            out_copy(side, n).wait()
    head_copy.wait()


def hand_over(*refs):
    sources, results, held, in_sems, out_sems = refs[:3], refs[3:6], refs[6:9], refs[9], refs[10]
    reads, writes = [], []
    for i, (src, dst, mid) in enumerate(zip(sources, results, held)):
        rows = src.shape[0] // SPLIT
        for n in range(SPLIT):
            part = pl.ds(n * rows, rows)
            reads.append(pltpu.make_async_copy(src.at[part], mid.at[part], in_sems.at[i, n]))
            writes.append(pltpu.make_async_copy(mid.at[part], dst.at[part], out_sems.at[i, n]))
    for read in reads:
        read.start()
    for read, write in zip(reads, writes):
        read.wait()
        write.start()
    for write in writes:
        write.wait()


def per_device(image, text, text_in, log_scale, bias):
    dma = pltpu.SemaphoreType.DMA
    vmem = pltpu.VMEM
    anywhere = pl.BlockSpec(memory_space=pl.ANY)
    scalars = pl.BlockSpec(memory_space=pltpu.SMEM)
    grads = pl.pallas_call(
        kernel,
        out_shape=(
            jax.ShapeDtypeStruct((ROWS, D), BF16),
            jax.ShapeDtypeStruct((ROWS, D), BF16),
            jax.ShapeDtypeStruct((HIN, HOUT), BF16),
        ),
        in_specs=[anywhere, anywhere, anywhere, scalars, scalars],
        out_specs=(anywhere, anywhere, anywhere),
        scratch_shapes=[
            vmem((2, ROWS, D), BF16),
            vmem((2, ROWS, 128), F32),
            vmem((2, ROWS, D), BF16),
            vmem((2, ROWS, D), F32),
            vmem((2, 2, NCH, CH, D), BF16),
            vmem((2, 2, NCH, CH, D), BF16),
            vmem((2, ROWS, D), BF16),
            vmem((HIN, ROWS), BF16),
            vmem((HALF, ROWS), BF16),
            vmem((ROWS, WIDE), BF16),
            vmem((HALF, WIDE), F32),
            vmem((192, 128), F32),
            vmem((NX, PIECE, 128), BF16),
            vmem((NX - 1, PIECE, 128), BF16),
            vmem((PADDED, 128), F32),
            vmem((PADDED, 128), BF16),
            vmem((NZ - 1, ZROWS, 128), BF16),
            vmem((ZROWS, 128), F32),
            vmem((NY, ZROWS, 128), F32),
            vmem((PADDED, 128), BF16),
            vmem((2, NX, PIECE, 128), BF16),
            vmem((HIN, HOUT), BF16),
            dma((3,)), dma((3, NCH)),
            dma((2, 2, NCH)), dma((2, 2, NCH)),
            dma((2, NCH)), dma((2, NCH)), dma((2, NCH)), dma((2, NCH)),
            dma((1,)), dma((1,)), dma((NCH,)), dma((NCH,)),
            dma((2, NX - 1)), dma((2, NX - 1)), dma((NZ - 1,)), dma((NZ - 1,)),
            dma((NY - 1,)), dma((NY - 1,)), dma((NZ - 1,)), dma((NZ - 1,)),
            dma((2, NX - 1)), dma((2, NX - 1)), dma((2, NX)), dma((2, NX)),
        ],
        compiler_params=pltpu.CompilerParams(
            collective_id=1, has_side_effects=True, vmem_limit_bytes=60 * 2**20
        ),
        cost_estimate=pl.CostEstimate(flops=7 * 10**9, bytes_accessed=5 * 10**6, transcendentals=2 * 10**6),
        name="band",
    )(image, text, text_in.T, log_scale, bias)
    return pl.pallas_call(
        hand_over,
        out_shape=tuple(jax.ShapeDtypeStruct(g.shape, g.dtype) for g in grads),
        in_specs=[anywhere] * 3,
        out_specs=(anywhere,) * 3,
        scratch_shapes=[vmem(g.shape, g.dtype) for g in grads] + [dma((3, SPLIT)), dma((3, SPLIT))],
        cost_estimate=pl.CostEstimate(flops=0, bytes_accessed=5 * 10**6, transcendentals=0),
        name="hand_over",
    )(*grads)


def solution(mesh):
    placed = (P("dp", None), P("dp", None), P("dp", None), P(), P())
    return jax.shard_map(
        per_device,
        mesh=mesh,
        in_specs=placed,
        out_specs=(P("dp", None), P("dp", None), P()),
        check_vma=False,
    )
```
